32 devices in a mesh: grid: 2 (over core), img: 16 (over z, y, x).
Axes of the slice: x: 2, y: 2, z: 4, core: 2. Of those that a mesh axis runs over, the one named last changes fastest.
Arguments:
- images: bfloat16 [128, 24, 24, 384], P('img', 'grid'), may hold values from -6 to 6
- cotangent: bfloat16 [128, 24, 24, 384], P('img', 'grid'), may hold values from -6 to 6
- image_group: int32 [128], P('img'), may hold values from 0 to 1
- row_order: int32 [2, 24], replicated, may hold values from 0 to 23, each once within a row
- keep_mask: int32 [128, 2, 2], P('img'), may hold values 0 or 1
- resample: float32 [2, 24, 13, 112], P(None, 'grid'), may hold values from -0.5 to 0.5
- filters: float32 [2, 112, 2, 384], P(None, None, None, 'img'), may hold values from -4.2 to 4.2
- filters_first: float32 [2, 112, 2, 384], P(None, None, None, 'img')
- filters_second: float32 [2, 112, 2, 384], P(None, None, None, 'img')
- expand: float32 [2, 384, 1536], P(None, 'img'), may hold values from -0.3125 to 0.3125
- expand_first: float32 [2, 384, 1536], P(None, 'img')
- expand_second: float32 [2, 384, 1536], P(None, 'img')
- shrink: float32 [2, 1536, 384], P(None, 'img'), may hold values from -0.25 to 0.25
- shrink_first: float32 [2, 1536, 384], P(None, 'img')
- shrink_second: float32 [2, 1536, 384], P(None, 'img')
- norm_params: float32 [2, 4, 384], P(None, None, 'img')
- norm_first: float32 [2, 4, 384], P(None, None, 'img')
- norm_second: float32 [2, 4, 384], P(None, None, 'img')
- mlp_bias: float32 [2, 1920], P(None, 'img'), may hold values from -1.8 to 1.8
- bias_first: float32 [2, 1920], P(None, 'img')
- bias_second: float32 [2, 1920], P(None, 'img')
Outputs:
- output: bfloat16 [128, 24, 24, 384], P('img', 'grid')
- image_grad: float32 [128, 24, 24, 384], P('img', 'grid')
- new_filters: float32 [2, 112, 2, 384], P(None, None, None, 'img')
- new_filters_first: float32 [2, 112, 2, 384], P(None, None, None, 'img')
- new_filters_second: float32 [2, 112, 2, 384], P(None, None, None, 'img')
- new_expand: float32 [2, 384, 1536], P(None, 'img')
- new_expand_first: float32 [2, 384, 1536], P(None, 'img')
- new_expand_second: float32 [2, 384, 1536], P(None, 'img')
- new_shrink: float32 [2, 1536, 384], P(None, 'img')
- new_shrink_first: float32 [2, 1536, 384], P(None, 'img')
- new_shrink_second: float32 [2, 1536, 384], P(None, 'img')
- new_norms: float32 [2, 4, 384], P(None, None, 'img')
- new_norm_first: float32 [2, 4, 384], P(None, None, 'img')
- new_norm_second: float32 [2, 4, 384], P(None, None, 'img')
- new_bias: float32 [2, 1920], P(None, 'img')
- new_bias_first: float32 [2, 1920], P(None, 'img')
- new_bias_second: float32 [2, 1920], P(None, 'img')
The draws below stay inside these ranges and needn't reach their ends.
Inputs may be any that keep to these rules, and one draw needn't show every extreme that they name: `row_order`: each row is a permutation of the 24 row slots.
All inputs are finite; a program needn't handle non-finite values. No bound on the sum of `keep_mask` on one device may be relied on, other than what follows from the above.
Results may differ from the reference program's by a relative error of at most 0.025.
Values may be sent and summed in bfloat16 or wider, within the bound.
A program may use at most 256 MiB of HBM per device.

```python
import math
import jax
import jax.numpy as jnp
from jax import lax

D = 384
FF = 1536
SIDE = 24
SIDE_LOW = 14
HALF = 13
BASE = 112
LAYERS = 2
STEP = 10
IMAGES = 128
TOKENS = 73728


def first_moment(key, shape, scale):
    return jax.random.normal(key, shape, jnp.float32) * (scale / 9.0)


def second_moment(key, shape, scale):
    unit = jax.random.uniform(key, shape, jnp.float32, 0.0, 1.0)
    return scale * scale * (1.0 / 999.0) * jnp.exp(unit * math.log(4.0))


def bias_scale():
    return jnp.concatenate([jnp.full((FF,), 0.3, jnp.float32), jnp.full((D,), 1.0, jnp.float32)]) * math.sqrt(TOKENS)


def draw_filters_first(key, part):
    key = jax.random.fold_in(key, 11)
    return first_moment(key, (LAYERS, BASE, 2, D), 3.0 * math.sqrt(IMAGES))


def draw_filters_second(key, part):
    key = jax.random.fold_in(key, 12)
    return second_moment(key, (LAYERS, BASE, 2, D), 3.0 * math.sqrt(IMAGES))


def draw_expand_first(key, part):
    key = jax.random.fold_in(key, 13)
    return first_moment(key, (LAYERS, D, FF), 0.3 * math.sqrt(TOKENS))


def draw_expand_second(key, part):
    key = jax.random.fold_in(key, 14)
    return second_moment(key, (LAYERS, D, FF), 0.3 * math.sqrt(TOKENS))


def draw_shrink_first(key, part):
    key = jax.random.fold_in(key, 15)
    return first_moment(key, (LAYERS, FF, D), 0.6 * math.sqrt(TOKENS))


def draw_shrink_second(key, part):
    key = jax.random.fold_in(key, 16)
    return second_moment(key, (LAYERS, FF, D), 0.6 * math.sqrt(TOKENS))


def draw_norm_params(key, part):
    key = jax.random.fold_in(key, 17)
    gain_key, shift_key = jax.random.split(key)
    gains = jax.random.uniform(gain_key, (LAYERS, 2, D), jnp.float32, 0.5, 1.5)
    shifts = jax.random.normal(shift_key, (LAYERS, 2, D), jnp.float32) * 0.3
    return jnp.stack([gains[:, 0], shifts[:, 0], gains[:, 1], shifts[:, 1]], axis=1)


def draw_norm_first(key, part):
    key = jax.random.fold_in(key, 18)
    return first_moment(key, (LAYERS, 4, D), 0.7 * math.sqrt(TOKENS))


def draw_norm_second(key, part):
    key = jax.random.fold_in(key, 19)
    return second_moment(key, (LAYERS, 4, D), 0.7 * math.sqrt(TOKENS))


def draw_bias_first(key, part):
    key = jax.random.fold_in(key, 20)
    return jax.random.normal(key, (LAYERS, FF + D), jnp.float32) * (bias_scale()[None, :] / 9.0)


def draw_bias_second(key, part):
    key = jax.random.fold_in(key, 21)
    unit = jax.random.uniform(key, (LAYERS, FF + D), jnp.float32, 0.0, 1.0)
    scale_row = bias_scale()[None, :]
    return scale_row * scale_row * (1.0 / 999.0) * jnp.exp(unit * math.log(4.0))


def place_ends(values, own_key, least, largest):
    extent = values.shape
    index_at = [jax.random.randint(jax.random.fold_in(own_key, axis), (), 0, extent[axis]) for axis in range(len(extent))]
    values = values.at[tuple(index_at)].set(least)
    longest = extent.index(max(extent))
    index_at[longest] = (index_at[longest] + 1) % extent[longest]
    return values.at[tuple(index_at)].set(largest)


def levels(key, dims, cuts, low, high):
    level = 1.0
    for position, shards_of in cuts:
        steps = jax.random.uniform(jax.random.fold_in(jax.random.fold_in(key, 6), position), (shards_of,), jnp.float32, low / len(cuts), high / len(cuts))
        level = level * jnp.repeat(jnp.exp(steps), dims[position] // shards_of).reshape((-1,) + (1,) * (len(dims) - 1 - position))
    return level


def noise(own_key, shape, spread, limit, cuts=(), kind=jnp.bfloat16):
    level = levels(own_key, shape, cuts, -0.22, 0.18) if cuts else 1.0
    drawn = jax.random.normal(own_key, shape, jnp.float32) * spread * level
    return jnp.minimum(jnp.maximum(drawn, -limit), limit).astype(kind)


def setup_inputs(seed: int = 0) -> dict:
    key_list = jax.random.split(jax.random.key(seed), 22)
    return {
        "images": noise(key_list[0], (IMAGES, SIDE, SIDE, D), 1.0, 6.0, ((0, 16), (1, 2))),
        "cotangent": noise(key_list[1], (IMAGES, SIDE, SIDE, D), 1.0, 6.0, ((0, 16), (1, 2))),
        "image_group": place_ends(jax.random.randint(key_list[2], (IMAGES,), 0, 2), jax.random.fold_in(key_list[2], 1), 0, 1).astype(jnp.int32),
        "row_order": jax.vmap(lambda own: jax.random.permutation(own, SIDE))(jax.random.split(key_list[3], 2)).reshape((2, SIDE)).astype(jnp.int32),
        "keep_mask": place_ends((jax.random.randint(key_list[4], (IMAGES, LAYERS, 2), 0, 8) < 7).astype(jnp.int32), jax.random.fold_in(key_list[4], 1), 0, 1),
        "resample": noise(key_list[5], (2, SIDE, HALF, BASE), BASE ** -0.5, 0.5, ((1, 2),), jnp.float32),
        "filters": noise(key_list[6], (LAYERS, BASE, 2, D), 0.7, 4.2, ((3, 16),), jnp.float32),
        "filters_first": draw_filters_first(jax.random.fold_in(key_list[21], 71), 0),
        "filters_second": draw_filters_second(jax.random.fold_in(key_list[21], 71), 0),
        "expand": noise(key_list[9], (LAYERS, D, FF), D ** -0.5, 0.3125, ((1, 16),), jnp.float32),
        "expand_first": draw_expand_first(jax.random.fold_in(key_list[21], 71), 0),
        "expand_second": draw_expand_second(jax.random.fold_in(key_list[21], 71), 0),
        "shrink": noise(key_list[12], (LAYERS, FF, D), (FF // 3) ** -0.5, 0.25, ((1, 16),), jnp.float32),
        "shrink_first": draw_shrink_first(jax.random.fold_in(key_list[21], 71), 0),
        "shrink_second": draw_shrink_second(jax.random.fold_in(key_list[21], 71), 0),
        "norm_params": draw_norm_params(jax.random.fold_in(key_list[21], 71), 0),
        "norm_first": draw_norm_first(jax.random.fold_in(key_list[21], 71), 0),
        "norm_second": draw_norm_second(jax.random.fold_in(key_list[21], 71), 0),
        "mlp_bias": noise(key_list[18], (LAYERS, FF + D), 0.3, 1.8, ((1, 16),), jnp.float32),
        "bias_first": draw_bias_first(jax.random.fold_in(key_list[21], 71), 0),
        "bias_second": draw_bias_second(jax.random.fold_in(key_list[21], 71), 0),
    }


@jax.custom_vjp
def low(v):
    return lax.optimization_barrier(v.astype(jnp.bfloat16)).astype(jnp.float32)

@jax.custom_vjp
def low_back(v):
    return v

def low_keep(v):
    return (low(v), None)

def low_pass(kept, grad):
    return (grad,)

def back_keep(v):
    return (v, None)

def back_low(kept, grad):
    return (low(grad),)
low.defvjp(low_keep, low_pass)
low_back.defvjp(back_keep, back_low)
NORM_EPS = 1e-06
DROP_RATES = (0.1, 0.15)
BETA_ONE = 0.9
BETA_TWO = 0.999
ADAM_EPS = 1e-08
LEARN_RATES = (0.5, 0.04, 0.02, 0.3, 0.2)
WEIGHT_DECAYS = (0.05, 0.05, 0.05, 0.0, 0.0)
HIGHEST = lax.Precision.HIGHEST

def phase_tables(slot_rows, height):
    freq_rows = jnp.arange(SIDE, dtype=jnp.int32)[:, None, None, None]
    freq_cols = jnp.arange(HALF, dtype=jnp.int32)[None, :, None, None]
    image_rows = slot_rows.astype(jnp.int32)[None, None, :, None]
    columns = jnp.arange(SIDE, dtype=jnp.int32)[None, None, None, :]
    phase_count = (freq_rows * image_rows + freq_cols * columns) % height
    angles = phase_count.astype(jnp.float32) * (2.0 * math.pi / height)
    live_mask = (freq_rows < height) & (freq_cols <= height // 2) & (image_rows < height) & (columns < height)
    live_value = live_mask.astype(jnp.float32)
    forward = jnp.stack([jnp.cos(angles) * live_value, -jnp.sin(angles) * live_value], axis=2)
    edge_cols = (freq_cols == 0) | (freq_cols == height // 2)
    col_weight = jnp.where(edge_cols, 1.0, 2.0).astype(jnp.float32) / (height * height)
    inverse = forward * col_weight[:, :, None, :, :]
    slot_count = slot_rows.shape[0]
    return (forward.reshape(2 * SIDE * HALF, slot_count * SIDE), inverse.reshape(2 * SIDE * HALF, slot_count * SIDE))

def layer_norm(values, gain, shift):
    mean_value = lax.optimization_barrier(jnp.mean(values, axis=-1, keepdims=True))
    centred = values - mean_value
    variance = lax.optimization_barrier(jnp.mean(centred * centred, axis=-1, keepdims=True))
    return centred * lax.rsqrt(variance + NORM_EPS) * gain + shift

def gelu_exact(values):
    return jax.nn.gelu(values, approximate=False)

def adamw(weight, first, second, grad, rate, decay):
    first_new = BETA_ONE * first + (1.0 - BETA_ONE) * grad
    second_new = BETA_TWO * second + (1.0 - BETA_TWO) * grad * grad
    first_hat = first_new / (1.0 - BETA_ONE ** STEP)
    second_hat = second_new / (1.0 - BETA_TWO ** STEP)
    weight_new = weight - rate * (first_hat / (jnp.sqrt(second_hat) + ADAM_EPS) + decay * weight)
    return (weight_new, first_new, second_new)

def reference(images, cotangent, image_group, row_order, keep_mask, resample, filters, filters_first, filters_second, expand, expand_first, expand_second, shrink, shrink_first, shrink_second, norm_params, norm_first, norm_second, mlp_bias, bias_first, bias_second):
    heights = (SIDE_LOW, SIDE)
    fwd_list = []
    inv_list = []
    for group_id in range(2):
        fwd_tab, inv_tab = phase_tables(row_order[group_id], heights[group_id])
        fwd_list.append(low(fwd_tab))
        inv_list.append(low(inv_tab))
    fwd_pair = jnp.stack(fwd_list)
    inv_pair = jnp.stack(inv_list)
    maps = resample.reshape(2, SIDE * HALF, BASE)
    rate_scale = jnp.array([1.0 / (1.0 - DROP_RATES[0]), 1.0 / (1.0 - DROP_RATES[1])], dtype=jnp.float32)
    keep_scale = keep_mask.astype(jnp.float32) * rate_scale[None, :, None]
    params = (filters, expand, shrink, norm_params, mlp_bias)
    block_count = 8
    blocks = IMAGES // block_count
    slots = 2 * SIDE * HALF

    def forward(params_in, block_images, block_group, block_keep):
        filt_p, expand_p, shrink_p, norm_p, bias_p = [low(p) for p in params_in]
        large = block_group == 1
        fwd_img = jnp.where(large[:, None, None], fwd_pair[1][None], fwd_pair[0][None])
        inv_img = jnp.where(large[:, None, None], inv_pair[1][None], inv_pair[0][None])
        residual = block_images
        for layer_id in range(LAYERS):
            normed_a = low(layer_norm(residual, norm_p[layer_id, 0], norm_p[layer_id, 1]))
            spec = low_back(jnp.einsum('bst,btd->bsd', fwd_img, normed_a, precision=HIGHEST))
            filt_grp = jnp.einsum('gsj,jqd->gsqd', maps, filt_p[layer_id], precision=HIGHEST)
            filt_img = jnp.where(large[:, None, None, None], filt_grp[1][None], filt_grp[0][None])
            spec4 = spec.reshape(block_count, SIDE * HALF, 2, D)
            real_part = spec4[:, :, 0] * filt_img[:, :, 0] - spec4[:, :, 1] * filt_img[:, :, 1]
            imag_part = spec4[:, :, 0] * filt_img[:, :, 1] + spec4[:, :, 1] * filt_img[:, :, 0]
            mixed_spec = low(jnp.stack([real_part, imag_part], axis=2).reshape(block_count, slots, D))
            mixer = low_back(jnp.einsum('bst,bsd->btd', inv_img, mixed_spec, precision=HIGHEST))
            middle = residual + block_keep[:, layer_id, 0][:, None, None] * mixer
            normed_b = low(layer_norm(middle, norm_p[layer_id, 2], norm_p[layer_id, 3]))
            pre = low_back(jnp.einsum('btd,df->btf', normed_b, expand_p[layer_id], precision=HIGHEST) + bias_p[layer_id, :FF])
            act = low(gelu_exact(pre))
            branch = low_back(jnp.einsum('btf,fd->btd', act, shrink_p[layer_id], precision=HIGHEST) + bias_p[layer_id, FF:])
            residual = middle + block_keep[:, layer_id, 1][:, None, None] * branch
        return residual

    def one_block(carry, inputs):
        block_images, block_cot, block_group, block_keep = inputs

        def tied(params_in, image_values):
            return forward(params_in, image_values, block_group, block_keep)
        result, pullback = jax.vjp(tied, params, block_images)
        grad_params, grad_images = pullback(block_cot)
        carry = jax.tree.map(jnp.add, carry, grad_params)
        return (carry, (result, grad_images))
    zeros = jax.tree.map(jnp.zeros_like, params)
    stacked = (images.astype(jnp.float32).reshape(blocks, block_count, SIDE * SIDE, D), cotangent.astype(jnp.float32).reshape(blocks, block_count, SIDE * SIDE, D), image_group.reshape(blocks, block_count), keep_scale.reshape(blocks, block_count, LAYERS, 2))
    totals, (results, grads) = lax.scan(one_block, zeros, stacked)
    output = results.reshape(IMAGES, SIDE, SIDE, D).astype(jnp.bfloat16)
    image_grad = grads.reshape(IMAGES, SIDE, SIDE, D)
    firsts = (filters_first, expand_first, shrink_first, norm_first, bias_first)
    seconds = (filters_second, expand_second, shrink_second, norm_second, bias_second)
    updated = []
    for index in range(5):
        updated.extend(adamw(params[index], firsts[index], seconds[index], totals[index], LEARN_RATES[index], WEIGHT_DECAYS[index]))
    return (output, image_grad, updated[0], updated[1], updated[2], updated[3], updated[4], updated[5], updated[6], updated[7], updated[8], updated[9], updated[10], updated[11], updated[12], updated[13], updated[14])
```

```python
import math

import jax
import jax.numpy as jnp
import ml_dtypes
import numpy as np
from jax import lax
from jax.experimental import pallas as pl
from jax.experimental.pallas import tpu as pltpu
from jax.sharding import PartitionSpec as P

SIDE = 24
SIDE_LOW = 14
HALF = 13
BASE = 112
LAYERS = 2
STEP = 10


NORM_EPS = 1e-06
DROP_RATES = (0.1, 0.15)
BETA_ONE = 0.9
BETA_TWO = 0.999
ADAM_EPS = 1e-08
LEARN_RATES = (0.5, 0.04, 0.02, 0.3, 0.2)
WEIGHT_DECAYS = (0.05, 0.05, 0.05, 0.0, 0.0)
HIGHEST = lax.Precision.HIGHEST


def phase_tables(slot_rows, height):
    freq_rows = jnp.arange(SIDE, dtype=jnp.int32)[:, None, None, None]
    freq_cols = jnp.arange(HALF, dtype=jnp.int32)[None, :, None, None]
    image_rows = slot_rows[None, None, :, None]
    columns = jnp.arange(SIDE, dtype=jnp.int32)[None, None, None, :]
    phase_count = (freq_rows * image_rows + freq_cols * columns) % height
    angles = phase_count.astype(jnp.float32) * (2.0 * math.pi / height)
    live_mask = (
        (freq_rows < height)
        & (freq_cols <= height // 2)
        & (image_rows < height)
        & (columns < height)
    )
    live_value = live_mask.astype(jnp.float32)
    forward = jnp.stack([jnp.cos(angles) * live_value, -jnp.sin(angles) * live_value], axis=2)
    edge_cols = (freq_cols == 0) | (freq_cols == height // 2)
    col_weight = jnp.where(edge_cols, 1.0, 2.0).astype(jnp.float32) / (height * height)
    inverse = forward * col_weight[:, :, None, :, :]
    slot_count = slot_rows.shape[0]
    return (
        forward.reshape(2 * SIDE * HALF, slot_count * SIDE),
        inverse.reshape(2 * SIDE * HALF, slot_count * SIDE),
    )


def layer_norm(values, gain, shift):
    mean_value = jnp.mean(values, axis=-1, keepdims=True)
    centred = values - mean_value
    variance = jnp.mean(centred * centred, axis=-1, keepdims=True)
    inv_std = lax.rsqrt(variance + NORM_EPS)
    normal = centred * inv_std
    return (normal * gain + shift, normal, inv_std)


def norm_back(grad_out, normal, inv_std, gain):
    scaled = grad_out * gain
    grad_in = inv_std * (
        scaled
        - jnp.mean(scaled, axis=-1, keepdims=True)
        - normal * jnp.mean(scaled * normal, axis=-1, keepdims=True)
    )
    return (grad_in, jnp.sum(grad_out * normal, axis=(0, 1)), jnp.sum(grad_out, axis=(0, 1)))


def gelu_exact(values):
    return jax.nn.gelu(values, approximate=False)


def adamw(weight, first, second, grad, rate, decay):
    first_new = BETA_ONE * first + (1.0 - BETA_ONE) * grad
    second_new = BETA_TWO * second + (1.0 - BETA_TWO) * grad * grad
    first_hat = first_new / (1.0 - BETA_ONE**STEP)
    second_hat = second_new / (1.0 - BETA_TWO**STEP)
    weight_new = weight - rate * (first_hat / (jnp.sqrt(second_hat) + ADAM_EPS) + decay * weight)
    return (weight_new, first_new, second_new)


def choose_group(image_group, pair):
    return jnp.where((image_group == 1)[:, None, None], pair[1][None], pair[0][None])


def body(
    images,
    cotangent,
    image_group,
    row_order,
    keep_mask,
    resample,
    filters,
    filters_first,
    filters_second,
    expand,
    expand_first,
    expand_second,
    shrink,
    shrink_first,
    shrink_second,
    norm_params,
    norm_first,
    norm_second,
    mlp_bias,
    bias_first,
    bias_second,
):
    count_img = images.shape[0]
    row_slots = images.shape[1]
    width = images.shape[3]
    local_tok = row_slots * SIDE
    half_local = resample.shape[1] * HALF
    spec_local = half_local * 2
    grid_index = lax.axis_index("grid")
    filt_all, expand_all, shrink_all, norm_all, bias_all = (
        lax.all_gather(filters.astype(jnp.bfloat16), "img", axis=3, tiled=True),
        lax.all_gather(expand.astype(jnp.bfloat16), "img", axis=1, tiled=True),
        lax.all_gather(shrink.astype(jnp.bfloat16), "img", axis=1, tiled=True),
        lax.all_gather(norm_params.astype(jnp.bfloat16), "img", axis=2, tiled=True),
        lax.all_gather(mlp_bias.astype(jnp.bfloat16), "img", axis=1, tiled=True),
    )
    hidden_units = expand_all.shape[2]
    heights = (SIDE_LOW, SIDE)
    fwd_list = []
    inv_list = []
    for group_id in range(2):
        slot_rows = lax.dynamic_slice_in_dim(row_order[group_id], grid_index * row_slots, row_slots)
        fwd_tab, inv_tab = phase_tables(slot_rows, heights[group_id])
        fwd_list.append(fwd_tab)
        inv_list.append(inv_tab)
    token_fwd = choose_group(image_group, jnp.stack(fwd_list).astype(jnp.bfloat16))
    token_inv = choose_group(image_group, jnp.stack(inv_list).astype(jnp.bfloat16))
    local_map = resample.reshape(2, half_local, BASE)
    selector = (image_group == 1)[None, None, :, None]
    member = jnp.stack([image_group == 0, image_group == 1], axis=1).astype(jnp.float32)
    rate_scale = jnp.array(
        [1.0 / (1.0 - DROP_RATES[0]), 1.0 / (1.0 - DROP_RATES[1])], dtype=jnp.float32
    )
    keep_scale = keep_mask.astype(jnp.float32) * rate_scale[None, :, None]
    norm_values = norm_all.astype(jnp.float32)
    bias_values = bias_all.astype(jnp.float32)
    residual = images.astype(jnp.float32).reshape(count_img, local_tok, width)
    saved = []
    for layer_id in range(LAYERS):
        normed_a, normal_a, inv_a = layer_norm(
            residual, norm_values[layer_id, 0], norm_values[layer_id, 1]
        )
        normed_a_low = normed_a.astype(jnp.bfloat16)
        spec = (
            lax.psum_scatter(
                jnp.einsum(
                    "ist,itd->sid", token_fwd, normed_a_low, preferred_element_type=jnp.float32
                ).astype(jnp.bfloat16),
                "grid",
                scatter_dimension=0,
                tiled=True,
            )
            .astype(jnp.float32)
            .reshape(half_local, 2, count_img, width)
        )
        filt_loc = jnp.einsum(
            "gsj,jqd->gsqd", local_map, filt_all[layer_id].astype(jnp.float32), precision=HIGHEST
        )
        filt_img = jnp.where(selector, filt_loc[1][:, :, None, :], filt_loc[0][:, :, None, :])
        real_part = spec[:, 0] * filt_img[:, 0] - spec[:, 1] * filt_img[:, 1]
        imag_part = spec[:, 0] * filt_img[:, 1] + spec[:, 1] * filt_img[:, 0]
        mixed_spec = (
            jnp.stack([real_part, imag_part], axis=1)
            .reshape(spec_local, count_img, width)
            .astype(jnp.bfloat16)
        )
        mixer = jnp.einsum(
            "ist,sid->itd",
            token_inv,
            lax.all_gather(mixed_spec, "grid", axis=0, tiled=True),
            preferred_element_type=jnp.float32,
        )
        mixer_scale = keep_scale[:, layer_id, 0][:, None, None]
        middle = residual + mixer_scale * mixer
        normed_b, normal_b, inv_b = layer_norm(
            middle, norm_values[layer_id, 2], norm_values[layer_id, 3]
        )
        normed_b_low = normed_b.astype(jnp.bfloat16)
        pre = (
            jnp.einsum(
                "itd,df->itf",
                normed_b_low,
                expand_all[layer_id],
                preferred_element_type=jnp.float32,
            )
            + bias_values[layer_id, :hidden_units]
        )
        act_low = gelu_exact(pre).astype(jnp.bfloat16)
        branch = (
            jnp.einsum(
                "itf,fd->itd", act_low, shrink_all[layer_id], preferred_element_type=jnp.float32
            )
            + bias_values[layer_id, hidden_units:]
        )
        mlp_scale = keep_scale[:, layer_id, 1][:, None, None]
        residual = middle + mlp_scale * branch
        saved.append(
            (
                normal_a,
                inv_a,
                normed_a_low,
                spec,
                filt_img,
                normal_b,
                inv_b,
                normed_b_low,
                pre,
                act_low,
            )
        )
    output = residual.astype(jnp.bfloat16).reshape(count_img, row_slots, SIDE, width)
    grad_up = cotangent.astype(jnp.float32).reshape(count_img, local_tok, width)
    grad_filters = [None] * LAYERS
    grad_expand = [None] * LAYERS
    grad_shrink = [None] * LAYERS
    grad_norms = [None] * LAYERS
    grad_bias = [None] * LAYERS
    for layer_id in range(LAYERS - 1, -1, -1):
        (
            normal_a,
            inv_a,
            normed_a_low,
            spec,
            filt_img,
            normal_b,
            inv_b,
            normed_b_low,
            pre,
            act_low,
        ) = saved[layer_id]
        mixer_scale = keep_scale[:, layer_id, 0][:, None, None]
        mlp_scale = keep_scale[:, layer_id, 1][:, None, None]
        grad_branch = (grad_up * mlp_scale).astype(jnp.bfloat16)
        grad_shrink[layer_id] = jnp.einsum(
            "itf,itd->fd", act_low, grad_branch, preferred_element_type=jnp.float32
        )
        bias_out = jnp.sum(grad_branch, axis=(0, 1), dtype=jnp.float32)
        d_act = jnp.einsum(
            "itd,fd->itf", grad_branch, shrink_all[layer_id], preferred_element_type=jnp.float32
        )
        gelu_pull = jax.vjp(gelu_exact, pre)[1]
        d_pre_low = gelu_pull(d_act)[0].astype(jnp.bfloat16)
        grad_expand[layer_id] = jnp.einsum(
            "itd,itf->df", normed_b_low, d_pre_low, preferred_element_type=jnp.float32
        )
        bias_hidden = jnp.sum(d_pre_low, axis=(0, 1), dtype=jnp.float32)
        d_normed_b = jnp.einsum(
            "itf,df->itd", d_pre_low, expand_all[layer_id], preferred_element_type=jnp.float32
        )
        d_middle, gain_b_grad, shift_b_grad = norm_back(
            d_normed_b, normal_b, inv_b, norm_values[layer_id, 2]
        )
        grad_mid = grad_up + d_middle
        grad_mixer = (grad_mid * mixer_scale).astype(jnp.bfloat16)
        d_mixed = (
            lax.psum_scatter(
                jnp.einsum(
                    "ist,itd->sid", token_inv, grad_mixer, preferred_element_type=jnp.float32
                ).astype(jnp.bfloat16),
                "grid",
                scatter_dimension=0,
                tiled=True,
            )
            .astype(jnp.float32)
            .reshape(half_local, 2, count_img, width)
        )
        d_real = d_mixed[:, 0]
        d_imag = d_mixed[:, 1]
        prod_real = d_real * spec[:, 0] + d_imag * spec[:, 1]
        prod_imag = d_imag * spec[:, 0] - d_real * spec[:, 1]
        group_terms = jnp.einsum(
            "ig,sqid->gsqd", member, jnp.stack([prod_real, prod_imag], axis=1), precision=HIGHEST
        )
        grad_filters[layer_id] = jnp.einsum(
            "gsj,gsqd->jqd", local_map, group_terms, precision=HIGHEST
        )
        spec_real = d_real * filt_img[:, 0] + d_imag * filt_img[:, 1]
        spec_imag = d_imag * filt_img[:, 0] - d_real * filt_img[:, 1]
        d_spec_low = (
            jnp.stack([spec_real, spec_imag], axis=1)
            .reshape(spec_local, count_img, width)
            .astype(jnp.bfloat16)
        )
        d_normed_a = jnp.einsum(
            "ist,sid->itd",
            token_fwd,
            lax.all_gather(d_spec_low, "grid", axis=0, tiled=True),
            preferred_element_type=jnp.float32,
        )
        d_input, gain_a_grad, shift_a_grad = norm_back(
            d_normed_a, normal_a, inv_a, norm_values[layer_id, 0]
        )
        grad_up = grad_mid + d_input
        grad_norms[layer_id] = jnp.stack(
            [gain_a_grad, shift_a_grad, gain_b_grad, shift_b_grad], axis=0
        )
        grad_bias[layer_id] = jnp.concatenate([bias_hidden, bias_out], axis=0)
    image_grad = grad_up.reshape(count_img, row_slots, SIDE, width)
    full_filters = jnp.stack(grad_filters)
    full_expand = jnp.stack(grad_expand)
    full_shrink = jnp.stack(grad_shrink)
    full_norms = jnp.stack(grad_norms)
    full_bias = jnp.stack(grad_bias)
    total_filters, total_expand, total_shrink, total_norms, total_bias = (
        lax.psum(full_filters.astype(jnp.bfloat16), "grid").astype(jnp.float32),
        lax.psum(full_expand.astype(jnp.bfloat16), "grid").astype(jnp.float32),
        lax.psum(full_shrink.astype(jnp.bfloat16), "grid").astype(jnp.float32),
        lax.psum(full_norms.astype(jnp.bfloat16), "grid").astype(jnp.float32),
        lax.psum(full_bias.astype(jnp.bfloat16), "grid").astype(jnp.float32),
    )
    summed = (
        lax.psum_scatter(
            total_filters.astype(jnp.bfloat16), "img", scatter_dimension=3, tiled=True
        ).astype(jnp.float32),
        lax.psum_scatter(
            total_expand.astype(jnp.bfloat16), "img", scatter_dimension=1, tiled=True
        ).astype(jnp.float32),
        lax.psum_scatter(
            total_shrink.astype(jnp.bfloat16), "img", scatter_dimension=1, tiled=True
        ).astype(jnp.float32),
        lax.psum_scatter(
            total_norms.astype(jnp.bfloat16), "img", scatter_dimension=2, tiled=True
        ).astype(jnp.float32),
        lax.psum_scatter(
            total_bias.astype(jnp.bfloat16), "img", scatter_dimension=1, tiled=True
        ).astype(jnp.float32),
    )
    weights = (filters, expand, shrink, norm_params, mlp_bias)
    firsts = (filters_first, expand_first, shrink_first, norm_first, bias_first)
    seconds = (filters_second, expand_second, shrink_second, norm_second, bias_second)
    updated = []
    for index in range(5):
        updated.extend(
            adamw(
                weights[index],
                firsts[index],
                seconds[index],
                summed[index],
                LEARN_RATES[index],
                WEIGHT_DECAYS[index],
            )
        )
    return (
        output,
        image_grad,
        updated[0],
        updated[1],
        updated[2],
        updated[3],
        updated[4],
        updated[5],
        updated[6],
        updated[7],
        updated[8],
        updated[9],
        updated[10],
        updated[11],
        updated[12],
        updated[13],
        updated[14],
    )


LANES = 128
TILE_ROWS = 96
SPEC_HALF = 160
SPEC_ROWS = 2 * SPEC_HALF
VMEM_BYTES = 64 * 1024 * 1024
MESH_IDS = pl.DeviceIdType.MESH
LOG2_PEAK = -0.5 * math.log2(2.0 * math.pi)
HALF_LOG2_E = 0.5 / math.log(2.0)
BEND = (
    0.7978695564437048,
    0.03639280919444424,
    -8.821938529071787e-05,
    -3.660006037905966e-05,
    1.4185332299791553e-06,
)


def natural_tables(parts):
    tables = []
    for height in (SIDE_LOW, SIDE):
        freq_rows = np.arange(SIDE)[:, None, None, None]
        freq_cols = np.arange(HALF)[None, :, None, None]
        image_rows = np.arange(SIDE)[None, None, :, None]
        columns = np.arange(SIDE)[None, None, None, :]
        angles = ((freq_rows * image_rows + freq_cols * columns) % height) * (2.0 * np.pi / height)
        live = (
            (freq_rows < height)
            & (freq_cols <= height // 2)
            & (image_rows < height)
            & (columns < height)
        )
        pair = np.stack([np.cos(angles) * live, -np.sin(angles) * live])
        pair = pair.reshape(2, parts, SIDE * HALF // parts, SIDE * SIDE)
        pair = np.pad(pair, ((0, 0), (0, 0), (0, SPEC_ROWS // parts - pair.shape[2]), (0, 0)))
        tables.append(pair.reshape(2 * SPEC_ROWS, SIDE * SIDE))
    return np.stack(tables).astype(ml_dtypes.bfloat16)


def slot_weights():
    weights = np.zeros((2, HALF), np.float32)
    for group, height in enumerate((SIDE_LOW, SIDE)):
        for freq in range(HALF):
            weights[group, freq] = (1.0 if freq in (0, height // 2) else 2.0) / (height * height)
    return weights


def place(device_index):
    return device_index // 4, device_index % 4


def plane_peer(spot, step):
    x, y = spot % 2, spot // 2
    return ((y + step // 2) % 2) * 2 + (x + step % 2) % 2


def greet(core, chip):
    z, spot = place(chip)
    barrier = pltpu.get_barrier_semaphore()
    peers = [(1 - core, chip)]
    for step in (1, 2, 3):
        peers.append((core, z * 4 + plane_peer(spot, step)))
        peers.append((core, ((z + step) % 4) * 4 + spot))
    for peer in peers:
        pl.semaphore_signal(barrier, inc=1, device_id=peer, device_id_type=MESH_IDS)
    return barrier, len(peers)


class Item:
    def __init__(self, number, block, level):
        self.number, self.block, self.level = number, block, level


class Gather:
    def __init__(self, core, chip, line, plane, sibling):
        self.core, self.chip = core, chip
        self.z, self.spot = place(chip)
        self.line_sems, self.plane_sems, self.sibling_sems = line, plane, sibling

    def level(self, step):
        return (self.z + 4 - step) % 4

    def copy(self, ref, sems, index, peer):
        return pltpu.make_async_remote_copy(
            src_ref=ref,
            dst_ref=ref,
            send_sem=sems[0].at[index],
            recv_sem=sems[1].at[index],
            device_id=peer,
            device_id_type=MESH_IDS,
        )

    def line(self, item, step):
        peer = (self.core, ((self.z + step) % 4) * 4 + self.spot)
        index = item.number * 3 + step - 1
        return self.copy(item.block(self.z, self.spot), self.line_sems, index, peer)

    def plane(self, item, step, turn):
        peer = (self.core, self.z * 4 + plane_peer(self.spot, turn))
        index = item.number * 12 + step * 3 + turn - 1
        block = item.block(self.level(step), self.spot)
        return self.copy(block, self.plane_sems, index, peer)

    def sibling(self, item, step):
        index = item.number * 4 + step
        peer = (1 - self.core, self.chip)
        return self.copy(item.level(self.level(step)), self.sibling_sems, index, peer)

    def begin_line(self, item):
        for step in (1, 2, 3):
            self.line(item, step).start()

    def begin_plane(self, item):
        for turn in (1, 2, 3):
            self.plane(item, 0, turn).start()

    def begin(self, item):
        self.begin_line(item)
        self.begin_plane(item)

    def forward(self, item, step):
        self.line(item, step).wait_recv()
        for turn in (1, 2, 3):
            self.plane(item, step, turn).start()

    def share(self, item, step):
        for turn in (1, 2, 3):
            self.plane(item, step, turn).wait_recv()
        self.sibling(item, step).start()

    def finish(self, item):
        for step in range(4):
            self.sibling(item, step).wait_recv()

    def drain(self, item):
        for step in range(4):
            if step:
                self.line(item, step).wait_send()
            for turn in (1, 2, 3):
                self.plane(item, step, turn).wait_send()
            self.sibling(item, step).wait_send()


def add(kind, *terms):
    total = terms[0].astype(jnp.float32)
    for term in terms[1:]:
        total = total + term.astype(jnp.float32)
    return total.astype(kind)


class Scatter:
    def __init__(self, core, chip, number, staged, near, plane, column, line, own, sums, sems):
        self.core, self.chip, self.number = core, chip, number
        self.z, self.spot = place(chip)
        self.staged, self.near, self.plane, self.column = staged, near, plane, column
        self.line, self.own, self.sums, self.sems = line, own, sums, sems

    def rows(self, core):
        part = self.near.shape[2]
        return pl.ds(pl.multiple_of(core * part, 16), part)

    def copy(self, source, target, index, peer):
        index += self.number * 8
        return pltpu.make_async_remote_copy(
            src_ref=source,
            dst_ref=target,
            send_sem=self.sems[0].at[index],
            recv_sem=self.sems[1].at[index],
            device_id=peer,
            device_id_type=MESH_IDS,
        )

    def to_near(self):
        other = 1 - self.core
        source = self.staged.at[:, :, self.rows(other)]
        return self.copy(source, self.near, 0, (other, self.chip))

    def to_plane(self, turn):
        target = plane_peer(self.spot, turn)
        source = self.near.at[:, target]
        return self.copy(
            source, self.plane.at[turn - 1], turn, (self.core, self.z * 4 + target)
        )

    def to_line(self, step):
        target = (self.z + step) % 4
        return self.copy(
            self.column.at[target],
            self.line.at[step - 1],
            3 + step,
            (self.core, target * 4 + self.spot),
        )

    def to_sums(self):
        return self.copy(self.own, self.sums, 7, (1 - self.core, self.chip))

    def begin(self):
        self.to_near().start()

    def add_near(self):
        self.to_near().wait_recv()
        rows = self.rows(self.core)

        def one(index, carry):
            level, spot = index // 4, index % 4
            mine = self.staged[level, spot, rows]
            self.near[level, spot] = add(mine.dtype, mine, self.near[level, spot])
            return carry

        lax.fori_loop(0, 16, one, 0)
        for turn in (1, 2, 3):
            self.to_plane(turn).start()

    def add_plane(self):
        for turn in (1, 2, 3):
            self.to_plane(turn).wait_recv()

        def one(level, carry):
            terms = [self.plane[turn, level] for turn in range(3)]
            self.column[level] = add(self.column.dtype, self.near[level, self.spot], *terms)
            return carry

        lax.fori_loop(0, 4, one, 0)
        for step in (1, 2, 3):
            self.to_line(step).start()

    def add_line(self, local_sem):
        for step in (1, 2, 3):
            self.to_line(step).wait_recv()
        terms = [self.line[step] for step in range(3)]
        total = add(jnp.float32, self.column[self.z], *terms)
        pieces = total.shape[0] // self.own.shape[0]
        if pieces > 1:
            height = total.shape[0] // pieces
            total = jnp.concatenate(
                [total[k * height : (k + 1) * height] for k in range(pieces)], axis=1
            )
        self.own[...] = total
        self.to_sums().start()
        self.keep(local_sem).start()

    def keep(self, local_sem):
        return pltpu.make_async_copy(self.own, self.sums, local_sem)

    def drain(self, local_sem, near=True):
        self.to_sums().wait_recv()
        if near:
            self.to_near().wait_send()
        for turn in (1, 2, 3):
            self.to_plane(turn).wait_send()
            self.to_line(turn).wait_send()
        self.to_sums().wait_send()
        self.keep(local_sem).wait()


class LateScatter(Scatter):
    def to_plane(self, turn):
        target = plane_peer(self.spot, turn)
        source = self.staged.at[:, target]
        return self.copy(
            source, self.plane.at[turn - 1], turn, (self.core, self.z * 4 + target)
        )

    def to_sibling(self):
        return self.copy(self.own, self.near, 0, (1 - self.core, self.chip))

    def begin(self):
        for turn in (1, 2, 3):
            self.to_plane(turn).start()

    def add_plane(self):
        for turn in (1, 2, 3):
            self.to_plane(turn).wait_recv()
        for level in range(4):
            terms = [self.plane[turn, level] for turn in range(3)]
            self.column[level] = add(self.column.dtype, self.staged[level, self.spot], *terms)
        for step in (1, 2, 3):
            self.to_line(step).start()

    def add_line(self):
        for step in (1, 2, 3):
            self.to_line(step).wait_recv()
        terms = [self.line[step] for step in range(3)]
        self.own[...] = add(jnp.float32, self.column[self.z], *terms)
        self.to_sibling().start()

    def finish(self, total, local_sem):
        self.to_sibling().wait()
        for turn in (1, 2, 3):
            self.to_plane(turn).wait_send()
            self.to_line(turn).wait_send()
        total[...] = self.own[...] + self.near[...]
        copy = pltpu.make_async_copy(total, self.sums, local_sem)
        copy.start()
        copy.wait()


GATHERED = LAYERS + 1
LOCAL_SEMS = 24


def train_kernel(
    groups, order, keep,
    images, cotangent, expand_own, shrink_own, filter_own, norm_own, bias_own, resample_own, factors, table_in,
    sums_expand, sums_shrink, small_sums, out, image_grad, stash,
    weights, smalls, maps, table, table_t, expand, filt_low, filt, norms, bias,
    image_in, cotangent_in, normals, specs, starts, middle, grad_middle, spec,
    inv_stds, acts, slopes, d_pre_pair, normed_pair, grad_pair,
    grad_expand, grad_shrink, grad_filters, grad_norms, grad_bias, near, plane, column, line, own_expand, own_shrink,
    map_rows_own, map_own, small_own, norm_tile, bias_tile,
    early_staged, early_near, early_plane, early_column, early_line, early_own, early_total,
    late_staged, late_near, late_plane, late_column, late_line, late_own, late_total,
    line_send, line_recv, plane_send, plane_recv, sibling_send, sibling_recv,
    scatter_send, scatter_recv, swap_send, swap_recv, local_sems,
):
    core, chip = lax.axis_index("grid"), lax.axis_index("img")
    z, spot = place(chip)
    other = 1 - core
    share = image_in.shape[0]
    rows = images.shape[1]
    width = images.shape[3]
    tokens = SIDE * SIDE
    hidden = expand.shape[2]
    owners = weights.shape[2] * weights.shape[3]
    part = width // owners
    quarters = hidden // width
    chunk = hidden // 2
    low = jnp.bfloat16

    greeting = greet(core, chip)
    image_staged = grad_middle.at[:, pl.ds(0, rows)]
    cotangent_staged = grad_middle.at[:, pl.ds(rows, rows)]
    image_mine = pltpu.make_async_copy(
        images.at[pl.ds(core * share, share)],
        image_in.at[:, pl.ds(core * rows, rows)],
        local_sems.at[0],
    )
    image_stage = pltpu.make_async_copy(
        images.at[pl.ds(other * share, share)], image_staged, local_sems.at[1]
    )
    cotangent_mine = pltpu.make_async_copy(
        cotangent.at[pl.ds(core * share, share)],
        cotangent_in.at[:, pl.ds(core * rows, rows)],
        local_sems.at[2],
    )
    cotangent_stage = pltpu.make_async_copy(
        cotangent.at[pl.ds(other * share, share)], cotangent_staged, local_sems.at[3]
    )
    for copy in (image_stage, image_mine, cotangent_stage, cotangent_mine):
        copy.start()
    norm_tile[...] = jnp.zeros_like(norm_tile)
    small_own[...] = jnp.zeros_like(small_own)
    bias_tile[...] = jnp.zeros_like(bias_tile)
    bias_part = bias_own.shape[1]
    bias_tile[:LAYERS, :bias_part] = bias_own[...]
    shifted = lax.broadcasted_iota(jnp.int32, (LANES, 2 * LANES), 1) == (
        lax.broadcasted_iota(jnp.int32, (LANES, 2 * LANES), 0) + chip * bias_part % LANES
    )
    window = dot(bias_tile[...].astype(low), shifted.astype(jnp.float32).astype(low))
    pieces = []
    for layer_id in range(LAYERS):
        norm_tile[:4, :part] = norm_own[layer_id]
        turned_norms = jnp.transpose(
            jnp.concatenate(
                [
                    jnp.zeros((BASE, LANES), jnp.float32),
                    norm_tile[...],
                    jnp.zeros((LANES - BASE - 8, LANES), jnp.float32),
                ],
                axis=0,
            )
        )[:part]
        small_own[:, :BASE] = filter_own[layer_id, 0]
        pieces.append(small_own[...] + turned_norms)
        small_own[:, :BASE] = filter_own[layer_id, 1]
        pieces.append(small_own[...])
    pieces += [window[:, :LANES], window[:, LANES:]]
    pieces.append(jnp.zeros((LANES - TILE_ROWS - 16, LANES), jnp.float32))
    block = jnp.concatenate(pieces, axis=0).astype(low)
    small_half = LANES // 2

    @pl.when(core == 0)
    def _():
        smalls[z, spot, 0] = block[:small_half]

    @pl.when(core == 1)
    def _():
        smalls[z, spot, 1] = block[small_half:]

    map_rows_own[...] = jnp.zeros_like(map_rows_own)
    for freq_row in range(rows):
        for freq_col in range(HALF):
            slot = freq_row * HALF + freq_col
            both = resample_own[freq_row, freq_col]
            for group in range(2):
                map_rows_own[group, slot : slot + 1, :BASE] = both[group : group + 1]
    for group in range(2):
        scaled = map_rows_own[group] * factors[group] + factors[2]
        map_own[group] = scaled.astype(low)
    map_rows = pl.ds(pl.multiple_of(core * SPEC_HALF, SPEC_HALF), SPEC_HALF)
    for group in range(2):
        maps[group, map_rows] = map_own[group]

    @pl.when(core == 0)
    def _():
        for layer_id in range(LAYERS):
            values = expand_own[layer_id]
            pieces = [values[:, q * width : (q + 1) * width] for q in range(quarters)]
            weights[0, layer_id, z, spot] = jnp.concatenate(pieces, axis=0).astype(low)

    @pl.when(core == 1)
    def _():
        for layer_id in range(LAYERS):
            weights[1, layer_id, z, spot] = shrink_own[layer_id].astype(low)

    pl.semaphore_wait(*greeting)
    sibling = (other, chip)
    gather = Gather(
        core, chip, (line_send, line_recv), (plane_send, plane_recv), (sibling_send, sibling_recv)
    )
    small_item = Item(
        0,
        lambda level, at: smalls.at[level, at, core],
        lambda level: smalls.at[level, :, core],
    )
    items = [
        Item(
            1 + layer_id,
            lambda level, at, layer_id=layer_id: weights.at[core, layer_id, level, at],
            lambda level, layer_id=layer_id: weights.at[core, layer_id, level],
        )
        for layer_id in range(LAYERS)
    ]

    def swap(index, source, target):
        return pltpu.make_async_remote_copy(
            src_ref=source,
            dst_ref=target,
            send_sem=swap_send.at[index],
            recv_sem=swap_recv.at[index],
            device_id=sibling,
            device_id_type=MESH_IDS,
        )

    half = pl.ds(core * rows, rows)
    image_swap = swap(0, image_staged, image_in.at[:, half])
    cotangent_swap = swap(1, cotangent_staged, cotangent_in.at[:, half])
    map_swap = swap(2, map_own, maps.at[:, map_rows])
    gather.begin(small_item)
    map_swap.start()
    image_stage.wait()
    image_swap.start()
    gather.begin(items[0])
    cotangent_stage.wait()
    cotangent_swap.start()

    for group in range(2):

        def order_rows(pair, carry, group=group):
            both = jnp.concatenate(
                [
                    table_in[group, order[group, 2 * pair + side]].astype(jnp.float32)
                    for side in range(2)
                ],
                axis=0,
            )
            span = pl.ds(pl.multiple_of(pair * 2 * SIDE, 16), 2 * SIDE)
            table_t[group, span] = both.astype(low)
            return carry

        lax.fori_loop(0, SIDE // 2, order_rows, 0)
        table[group] = jnp.transpose(table_t[group])

    for step in (1, 2, 3):
        gather.forward(small_item, step)
    image_mine.wait()
    image_swap.wait_recv()

    def unpack_expand(layer_id):
        def take(pair, carry):
            level, at = pair // 2, pair % 2 * 2
            first = weights[0, layer_id, level, at].astype(jnp.float32)
            second = weights[0, layer_id, level, at + 1].astype(jnp.float32)
            span = pl.ds(pl.multiple_of(2 * part * pair, 16), 2 * part)
            for quarter in range(quarters):
                at_rows = slice(quarter * part, (quarter + 1) * part)
                both = jnp.concatenate([first[at_rows], second[at_rows]], axis=0)
                expand[layer_id, span, quarter * width : (quarter + 1) * width] = both.astype(low)
            return carry

        lax.fori_loop(0, owners // 2, take, 0)

    def norm_row(layer_id, index):
        return norms[layer_id, 4 + index : 5 + index, :]

    def filters_at(layer_id, group, at):
        return [filt[layer_id, group, side, at] for side in range(2)]

    def shrink_part(layer_id, piece):
        return weights[1, layer_id, 2 * piece : 2 * piece + 2].reshape(chunk, width)

    def expand_part(layer_id, piece):
        return expand[layer_id, :, piece * chunk : (piece + 1) * chunk]

    def load(source, index, at):
        lines = slice(at.start // SIDE, at.stop // SIDE)
        return source[index, lines].astype(jnp.float32).reshape(at.stop - at.start, width)

    def store(target, index, at, values):
        lines = slice(at.start // SIDE, at.stop // SIDE)
        target[index, lines] = values.reshape((at.stop - at.start) // SIDE, SIDE, width).astype(low)

    token_spans = spans(tokens, 2 * SIDE)
    slot_spans = spans(SPEC_ROWS, 32)

    def imag(at):
        return slice(at.start + SPEC_ROWS, at.stop + SPEC_ROWS)

    def group_of(index):
        return groups[core * share + index]

    def scale_of(index, layer_id, branch):
        kept = keep[layer_id, branch, core * share + index].astype(jnp.float32)
        return kept * (1.0 / (1.0 - DROP_RATES[layer_id]))

    def taken(source, index):
        return lambda at: [source[index, part] for part in (at, imag(at))]

    def spectrum_of_normed(layer_id, group, at, values):
        values = values * norm_row(layer_id, 0)
        if at.start:
            return values
        height = jnp.where(group == 1, float(SIDE * SIDE), float(SIDE_LOW * SIDE_LOW))
        first = lax.broadcasted_iota(jnp.int32, (8, 1), 0) == 0
        top = values[:8] + jnp.where(first, height, 0.0) * norm_row(layer_id, 1)
        return jnp.concatenate([top, values[8:]], axis=0)

    def unmix(layer_id, group, take):
        mixed_real, mixed_imag = [], []
        for at in slot_spans:
            real, imag_part = take(at)
            f_real, f_imag = filters_at(layer_id, group, at)
            mixed_real.append(real * f_real - imag_part * f_imag)
            mixed_imag.append(real * f_imag + imag_part * f_real)
        return dot_low(table_t[group], stack_rows(mixed_real + mixed_imag))

    def mix_back(layer_id, group, scale, normal_at, take, grad_at, put):
        low_grad = stack_rows([(grad_at(at) * scale).astype(low) for at in token_spans])
        both = dot_low(table[group], low_grad)
        prods, d_specs = ([], []), ([], [])
        for at in slot_spans:
            d_real, d_imag = both[at], both[imag(at)]
            real, imag_part = take(at)
            prods[0].append(d_real * real + d_imag * imag_part)
            prods[1].append(d_imag * real - d_real * imag_part)
            f_real, f_imag = filters_at(layer_id, group, at)
            d_specs[0].append(d_real * f_real + d_imag * f_imag)
            d_specs[1].append(d_imag * f_real - d_real * f_imag)
        for side in range(2):
            grad_filters[2 * layer_id + side] += dot_rows(stack_rows(prods[side]), maps[group])
        d_normed = dot_low(table_t[group], stack_rows(d_specs[0] + d_specs[1]))
        gain = norm_row(layer_id, 0)
        sums = [jnp.zeros((8, width), jnp.float32)] * 2
        for at in token_spans:
            normal, inv_std = normal_at(at)
            step = d_normed[at].astype(jnp.float32)
            sums = [sums[0] + row_sums(step * normal), sums[1] + row_sums(step)]
            put(at, grad_at(at) + norm_pull(step, normal, inv_std, gain))
        grad_norms[layer_id, 0] += sums[0]
        grad_norms[layer_id, 1] += sums[1]

    def hidden_part(layer_id, piece, normed):
        span = slice(piece * chunk, (piece + 1) * chunk)
        pre = dot_low(normed, expand_part(layer_id, piece))
        shift = bias[layer_id : layer_id + 1, span].astype(low)
        pairs = [gelu_pair(pre[at] + shift) for at in spans(tokens, 32)]
        return stack_rows([pair[0] for pair in pairs]), stack_rows([pair[1] for pair in pairs])

    def normed_for_feed(layer_id, values_at):
        gain, shift = norm_row(layer_id, 2), norm_row(layer_id, 3)
        kept = [normalise(values_at(at)) for at in token_spans]
        normed = stack_rows([(normal * gain + shift).astype(low) for normal, _ in kept])
        return kept, normed

    def turned_of(pair):
        return jnp.transpose(pair[...].reshape(2 * tokens, width))

    def add_expand(layer_id):
        turned = jnp.concatenate([turned_of(normed_pair), jnp.ones((16, 2 * tokens), low)], axis=0)
        for piece in range(3):
            span = slice(piece * hidden // 3, (piece + 1) * hidden // 3)
            both = dot(turned, d_pre_pair[:, :, span].reshape(2 * tokens, hidden // 3))
            accumulate(grad_expand, span, both)
            grad_bias[layer_id : layer_id + 1, span] += both[width : width + 1]

    def add_shrink(target, turned, acts_of):
        for piece in range(3):
            span = slice(piece * hidden // 3, (piece + 1) * hidden // 3)
            both = dot(turned, acts_of[:, :, span].reshape(2 * tokens, hidden // 3))
            accumulate(target, span, both)

    def branch_grad(layer_id, scale, grad_at):
        pieces = []
        total = jnp.zeros((8, width), jnp.float32)
        for at in token_spans:
            piece = (grad_at(at) * scale).astype(low)
            total = total + row_sums(piece.astype(jnp.float32))
            pieces.append(piece)
        grad_bias[layer_id : layer_id + 1, hidden : hidden + width] += jnp.sum(
            total, axis=0, keepdims=True
        )
        return stack_rows(pieces)

    def accumulate(target, span, values):
        for at in spans(width, 48):
            target[at, span] += values[at]

    def hidden_back(layer_id, piece, slope, grad_low, slot):
        span = slice(piece * chunk, (piece + 1) * chunk)
        d_act = dot_lanes(grad_low, shrink_part(layer_id, piece), low)
        d_pre = stack_rows([d_act[at] * slope[at] for at in spans(tokens, 32)])
        d_pre_pair[slot, :, span] = d_pre
        return dot_lanes(d_pre, expand_part(layer_id, piece))

    def feed_pull(layer_id, kept, steps, grad_at, put):
        gain = norm_row(layer_id, 2)
        sums = [jnp.zeros((8, width), jnp.float32)] * 2
        for at, (normal, inv_std) in zip(token_spans, kept):
            step = steps[0][at]
            for more in steps[1:]:
                step = step + more[at]
            sums = [sums[0] + row_sums(step * normal), sums[1] + row_sums(step)]
            put(at, grad_at(at) + norm_pull(step, normal, inv_std, gain))
        grad_norms[layer_id, 2] += sums[0]
        grad_norms[layer_id, 3] += sums[1]

    def first_spectra(index, carry):
        normals = [normalise(load(image_in, index, at))[0].astype(low) for at in token_spans]
        specs[index] = dot_low(table[group_of(index)], stack_rows(normals))

        @pl.when(index == 0)
        def _():
            for step in range(4):
                gather.share(small_item, step)
            gather.forward(items[0], 1)

        @pl.when(index == 1)
        def _():
            gather.forward(items[0], 2)

        @pl.when(index == 2)
        def _():
            gather.forward(items[0], 3)
            gather.begin_line(items[1])

        return carry

    lax.fori_loop(0, share, first_spectra, 0)
    for total in (grad_filters, grad_norms, grad_bias):
        total[...] = jnp.zeros_like(total)
    map_swap.wait_recv()
    gather.finish(small_item)

    bias[...] = jnp.zeros_like(bias)
    for pair in range(owners // 2):
        blocks = [
            smalls[(2 * pair + side) // 4, (2 * pair + side) % 4]
            .reshape(LANES, LANES)
            .astype(jnp.float32)
            for side in range(2)
        ]
        for index in range(2 * LAYERS):
            span = slice(index * part, (index + 1) * part)
            both = jnp.concatenate([block[span] for block in blocks], axis=0)
            filt_low[index, 2 * part * pair : 2 * part * (pair + 1)] = both.astype(low)
        for side in range(2):
            start = (2 * pair + side) * (hidden + width) // owners // LANES * LANES
            piece = blocks[side][TILE_ROWS : TILE_ROWS + 16]
            bias[:, start : start + LANES] += piece[:8]
            bias[:, start + LANES : start + 2 * LANES] += piece[8:]
    for layer_id in range(LAYERS):
        for group in range(2):
            for side in range(2):
                values = dot_lanes(maps[group], filt_low[2 * layer_id + side])
                filt[layer_id, group, side] = values.astype(low)
                if group == 0 and side == 0:
                    norms[layer_id] = values[SPEC_HALF - 8 : SPEC_HALF]

    def first_mix(index, carry):
        group = group_of(index)
        scale = scale_of(index, 0, 0)

        def take(at):
            pair = []
            for part_at in (at, imag(at)):
                values = specs[index, part_at].astype(jnp.float32)
                values = spectrum_of_normed(0, group, part_at, values).astype(low)
                specs[index, part_at] = values
                pair.append(values)
            return pair

        mixer = unmix(0, group, take)
        for at in token_spans:
            starts[index, at] = load(image_in, index, at) + scale * mixer[at]
        for step in range(4):

            @pl.when(index == step)
            def _(step=step):
                gather.share(items[0], step)

        return carry

    lax.fori_loop(0, share, first_mix, 0)
    gather.begin_plane(items[1])
    for step in (1, 2, 3):
        gather.forward(items[1], step)
    gather.finish(items[0])
    unpack_expand(0)

    def stash_out(index):
        copies = [
            pltpu.make_async_copy(slopes.at[index % 2], stash.at[2 + index], local_sems.at[4 + index])
        ]
        if index < 2:
            copies.append(
                pltpu.make_async_copy(acts.at[index], stash.at[index], local_sems.at[20 + index])
            )
        return copies

    def act_back(slot):
        return pltpu.make_async_copy(stash.at[slot], acts.at[slot], local_sems.at[8 + slot])

    def slope_back(index):
        return pltpu.make_async_copy(
            stash.at[2 + index], slopes.at[index % 2], local_sems.at[10 + index % 2]
        )

    def first_feed(index, carry):
        slot = index % 2
        kept, normed = normed_for_feed(0, lambda at: starts[index, at])
        for at in range(2):

            @pl.when(index == 2 + at)
            def _(at=at):
                for copy in stash_out(at):
                    copy.wait()

        branches = []
        for piece in range(2):
            span = slice(piece * chunk, (piece + 1) * chunk)
            act, slope = hidden_part(0, piece, normed)
            acts[slot, :, span] = act
            slopes[slot, :, span] = slope
            branches.append(dot(act, shrink_part(0, piece)))
        scale = scale_of(index, 0, 1)
        shift = bias[0:1, hidden : hidden + width]
        for at, (normal, inv_std) in zip(token_spans, kept):
            branch = branches[0][at] + branches[1][at] + shift
            starts[index, at] += scale * branch
            normals[index, at] = normal.astype(low)
            inv_stds[index, at] = inv_std
        for at in range(4):

            @pl.when(index == at)
            def _(at=at):
                for copy in stash_out(at):
                    copy.start()

        for at, steps in ((1, (0,)), (2, (1,)), (3, (2, 3))):

            @pl.when(index == at)
            def _(steps=steps):
                for step in steps:
                    gather.share(items[1], step)

        return carry

    lax.fori_loop(0, share, first_feed, 0)
    cotangent_mine.wait()
    image_swap.wait_send()
    cotangent_swap.wait_send()
    cotangent_swap.wait_recv()

    for total in (grad_expand, grad_shrink):
        total[...] = jnp.zeros_like(total)

    def second(turn, slot):
        index = (2 * turn + 2) % 4 + slot
        group = group_of(index)
        scale = scale_of(index, 1, 0)
        gain, shift = norm_row(1, 0), norm_row(1, 1)
        normed = stack_rows(
            [(normalise(starts[index, at])[0] * gain + shift).astype(low) for at in token_spans]
        )
        spec[index] = dot_low(table[group], normed)
        take = taken(spec, index)
        mixer = unmix(1, group, take)
        for at in token_spans:
            middle[at] = starts[index, at] + scale * mixer[at]
        scale = scale_of(index, 1, 1)
        kept, normed = normed_for_feed(1, lambda at: middle[at])
        normed_pair[slot] = normed
        grad_low = branch_grad(1, scale, lambda at: load(cotangent_in, index, at))
        grad_pair[slot] = grad_low
        branches, steps = [], []
        for piece in range(2):
            span = slice(piece * chunk, (piece + 1) * chunk)
            act, slope = hidden_part(1, piece, normed)
            slopes[slot, :, span] = act
            branches.append(dot(act, shrink_part(1, piece)))
            steps.append(hidden_back(1, piece, slope, grad_low, slot))
        shift = bias[1:2, hidden : hidden + width]

        def put_grad(at, values):
            branch = branches[0][at] + branches[1][at] + shift
            store(cotangent_in, index, at, middle[at] + scale * branch)
            store(grad_middle, index, at, values)

        feed_pull(1, kept, steps, lambda at: load(cotangent_in, index, at), put_grad)

    def seconds(turn, carry):
        def one(slot, inner):
            second(turn, slot)
            return inner

        lax.fori_loop(0, 2, one, 0)
        add_shrink(grad_shrink, turned_of(grad_pair), slopes)
        add_expand(1)
        return carry

    gather.finish(items[1])
    unpack_expand(1)
    for index in (2, 3):
        for copy in stash_out(index):
            copy.wait()
    lax.fori_loop(0, 2, seconds, 0)
    for index in (2, 3):
        slope_back(index).start()
    gather.drain(small_item)
    gather.drain(items[0])
    gather.drain(items[1])
    map_swap.wait_send()

    rest = pl.ds(other * rows, rows)
    home = pl.ds(core * share, share)

    def send_home(number, source, target):
        return (
            swap(3 + number, source.at[:, rest], target.at[home]),
            pltpu.make_async_copy(source.at[:, half], target.at[home], local_sems.at[12 + number]),
        )

    for copy in send_home(0, cotangent_in, out):
        copy.start()

    def stage_expand(layer_id):
        def put(owner, carry):
            values = grad_expand[pl.ds(pl.multiple_of(owner * part, 8), part), :]
            pieces = [values[:, q * width : (q + 1) * width] for q in range(quarters)]
            weights[0, layer_id, owner // 4, owner % 4] = jnp.concatenate(pieces, axis=0).astype(low)
            return carry

        lax.fori_loop(0, owners, put, 0)

    def stage_shrink(grad, staged):
        for level in range(4):
            span = slice(level * hidden // 4, (level + 1) * hidden // 4)
            flat = jnp.transpose(grad[:, span].astype(low))
            staged[level] = flat.reshape(4, TILE_ROWS, width)

    sems = (scatter_send, scatter_recv)
    half_width = pl.ds(pl.multiple_of(core * hidden // 2, 128), hidden // 2)
    half_rows = pl.ds(pl.multiple_of(core * TILE_ROWS // 2, 8), TILE_ROWS // 2)

    def scatter_expand(number, layer_id):
        return Scatter(
            core, chip, number, weights.at[0, layer_id],
            near.at[number], plane.at[number], column.at[number], line.at[number],
            own_expand.at[layer_id], sums_expand.at[layer_id, :, half_width], sems,
        )

    def scatter_shrink(number, layer_id, staged):
        return Scatter(
            core, chip, number, staged,
            near.at[number], plane.at[number], column.at[number], line.at[number],
            own_shrink.at[layer_id], sums_shrink.at[layer_id, half_rows], sems,
        )

    expand_second, shrink_second = scatter_expand(0, 1), scatter_shrink(1, 1, weights.at[1, 1])
    expand_first, shrink_first = scatter_expand(2, 0), scatter_shrink(3, 0, weights.at[0, 0])
    tail = 2 * part
    early_scatter = LateScatter(
        core, chip, 4, early_staged, early_near, early_plane, early_column, early_line, early_own,
        small_sums.at[pl.ds(tail, early_own.shape[0])], sems,
    )
    late_scatter = LateScatter(
        core, chip, 5, late_staged, late_near, late_plane, late_column, late_line, late_own,
        small_sums.at[pl.ds(0, tail)], sems,
    )

    def stage_smalls(layer_id, staged, with_bias):
        lanes = [jnp.zeros((BASE, width), jnp.float32)]
        lanes += [jnp.sum(grad_norms[layer_id, m], axis=0, keepdims=True) for m in range(4)]
        lanes.append(jnp.zeros((LANES - BASE - 4, width), jnp.float32))
        grad_filters[2 * layer_id] += jnp.transpose(jnp.concatenate(lanes, axis=0))
        for owner in range(owners):
            span = slice(owner * part, (owner + 1) * part)
            start = owner * (hidden + width) // owners // LANES * LANES
            blocks = [grad_filters[2 * layer_id + side, span] for side in range(2)]
            if with_bias:
                blocks.append(grad_bias[:, start : start + LANES])
                blocks.append(grad_bias[:, start + LANES : start + 2 * LANES])
            staged[owner // 4, owner % 4] = jnp.concatenate(blocks, axis=0).astype(low)

    stage_expand(1)
    expand_second.begin()
    stage_shrink(grad_shrink, weights.at[1, 1])
    shrink_second.begin()

    grad_shrink[...] = jnp.zeros_like(grad_shrink)

    def second_back(turn, slot):
        index = (2 * turn + 2) % 4 + slot

        def put_start(at, values):
            starts[index, at] = values

        mix_back(
            1, group_of(index), scale_of(index, 1, 0),
            lambda at: normalise(starts[index, at]), taken(spec, index),
            lambda at: load(grad_middle, index, at), put_start,
        )

    def second_backs(turn, carry):
        def one(slot, inner):
            second_back(turn, slot)
            return inner

        lax.fori_loop(0, 2, one, 0)

        @pl.when(turn == 0)
        def _():
            expand_second.add_near()
            shrink_second.add_near()

        @pl.when(turn == 1)
        def _():
            for slot in range(2):
                act_back(slot).wait()

        base = (2 * turn + 2) % 4
        grads = [
            branch_grad(
                0,
                scale_of(base + slot, 0, 1),
                lambda at, slot=slot: starts[base + slot, at],
            )
            for slot in range(2)
        ]
        add_shrink(grad_shrink, jnp.transpose(stack_rows(grads)), acts)

        @pl.when(turn == 0)
        def _():
            for slot in range(2):
                act_back(slot).start()

        return carry

    lax.fori_loop(0, 2, second_backs, 0)
    stage_shrink(grad_shrink, weights.at[0, 0])
    shrink_first.begin()

    grad_expand[...] = jnp.zeros_like(grad_expand)

    def first_feed_back(turn, slot):
        index = (2 * turn + 2) % 4 + slot
        scale = scale_of(index, 0, 1)
        gain, shift = norm_row(0, 2), norm_row(0, 3)
        kept = [(normals[index, at].astype(jnp.float32), inv_stds[index, at]) for at in token_spans]
        for at, (normal, _) in zip(token_spans, kept):
            normed_pair[slot, at] = (normal * gain + shift).astype(low)
        grad_low = stack_rows([(starts[index, at] * scale).astype(low) for at in token_spans])
        steps = []
        for piece in range(2):
            span = slice(piece * chunk, (piece + 1) * chunk)
            steps.append(hidden_back(0, piece, slopes[slot, :, span], grad_low, slot))

        def put_start(at, values):
            starts[index, at] = values

        feed_pull(0, kept, steps, lambda at: starts[index, at], put_start)

    def first_feed_backs(turn, carry):
        for at in range(2):

            @pl.when(turn == at)
            def _(at=at):
                for slot in range(2):
                    slope_back(2 * (1 - at) + slot).wait()

        def one(slot, inner):
            first_feed_back(turn, slot)

            @pl.when(turn + slot == 0)
            def _():
                shrink_first.add_near()

            return inner

        lax.fori_loop(0, 2, one, 0)

        @pl.when(turn == 0)
        def _():
            for slot in range(2):
                slope_back(slot).start()

        add_expand(0)

        @pl.when(turn == 0)
        def _():
            expand_second.add_plane()
            shrink_second.add_plane()

        @pl.when(turn == 1)
        def _():
            shrink_first.add_plane()

        return carry

    lax.fori_loop(0, 2, first_feed_backs, 0)
    shrink_first.to_near().wait_send()
    stage_expand(0)
    expand_first.begin()
    stage_smalls(1, early_staged, True)
    early_scatter.begin()

    def first_mix_back(index, carry):
        def take(at):
            return [specs[index, part_at] for part_at in (at, imag(at))]

        def put_image(at, values):
            store(image_in, index, at, values)

        mix_back(
            0, group_of(index), scale_of(index, 0, 0),
            lambda at: normalise(load(image_in, index, at)), take,
            lambda at: starts[index, at], put_image,
        )

        @pl.when(index == 0)
        def _():
            expand_first.add_near()

        @pl.when(index == 1)
        def _():
            expand_second.add_line(local_sems.at[14])
            shrink_second.add_line(local_sems.at[15])

        @pl.when(index == 2)
        def _():
            early_scatter.add_plane()

        @pl.when(index == 3)
        def _():
            early_scatter.add_line()

        return carry

    lax.fori_loop(0, share, first_mix_back, 0)
    for copy in send_home(1, image_in, image_grad):
        copy.start()

    stage_smalls(0, late_staged, False)
    late_scatter.begin()
    shrink_first.add_line(local_sems.at[16])
    expand_first.add_plane()
    late_scatter.add_plane()
    expand_first.add_line(local_sems.at[17])
    late_scatter.add_line()
    for number, (source, target) in enumerate(((cotangent_in, out), (image_in, image_grad))):
        for copy in send_home(number, source, target):
            copy.wait()
    expand_second.drain(local_sems.at[14])
    shrink_second.drain(local_sems.at[15])
    shrink_first.drain(local_sems.at[16], near=False)
    expand_first.drain(local_sems.at[17])
    early_scatter.finish(early_total, local_sems.at[18])
    late_scatter.finish(late_total, local_sems.at[19])


def train(
    groups, order, keep, images, cotangent, expand, shrink, filters, norms, biases, maps, factors, table
):
    count, rows, _, width = images.shape
    share = count // 2
    tokens = SIDE * SIDE
    hidden = expand.shape[2]
    low, full = jnp.bfloat16, jnp.float32
    block = (TILE_ROWS, width)
    half = (TILE_ROWS // 2, width)
    small = (LANES // 2, LANES)
    anywhere = pl.BlockSpec(memory_space=pl.ANY)
    inside = pl.BlockSpec(memory_space=pltpu.VMEM)
    scalar = pl.BlockSpec(memory_space=pltpu.SMEM)
    whole = (share, SIDE, SIDE, width)
    sems = pltpu.SemaphoreType.DMA

    def late_buffers(height):
        small = (height, LANES)
        return (
            pltpu.VMEM((4, 4) + small, low),
            pltpu.VMEM(small, full),
            pltpu.VMEM((3, 4) + small, low),
            pltpu.VMEM((4,) + small, low),
            pltpu.VMEM((3,) + small, low),
            pltpu.VMEM(small, full),
            pltpu.VMEM(small, full),
        )

    return pl.pallas_call(
        train_kernel,
        out_shape=(
            jax.ShapeDtypeStruct(expand.shape, full),
            jax.ShapeDtypeStruct(shrink.shape, full),
            jax.ShapeDtypeStruct((TILE_ROWS + 16, LANES), full),
            jax.ShapeDtypeStruct(images.shape, low),
            jax.ShapeDtypeStruct(images.shape, low),
            jax.ShapeDtypeStruct((6, tokens, hidden), low),
        ),
        in_specs=[scalar] * 3 + [anywhere] * 2 + [inside] * 8,
        out_specs=[anywhere] * 6,
        scratch_shapes=[
            pltpu.VMEM((2, LAYERS, 4, 4) + block, low),
            pltpu.VMEM((4, 4, 2) + small, low),
            pltpu.VMEM((2, SPEC_ROWS, LANES), low),
            pltpu.VMEM((2, 2 * SPEC_ROWS, tokens), low),
            pltpu.VMEM((2, tokens, 2 * SPEC_ROWS), low),
            pltpu.VMEM((LAYERS, width, hidden), low),
            pltpu.VMEM((2 * LAYERS, width, LANES), low),
            pltpu.VMEM((LAYERS, 2, 2, SPEC_ROWS, width), low),
            pltpu.VMEM((LAYERS, 8, width), full),
            pltpu.VMEM((8, 2048), full),
            pltpu.VMEM(whole, low),
            pltpu.VMEM(whole, low),
            pltpu.VMEM((share, tokens, width), low),
            pltpu.VMEM((share, 2 * SPEC_ROWS, width), low),
            pltpu.VMEM((share, tokens, width), full),
            pltpu.VMEM((tokens, width), full),
            pltpu.VMEM(whole, low),
            pltpu.VMEM((share, 2 * SPEC_ROWS, width), low),
            pltpu.VMEM((share, tokens, 1), full),
            pltpu.VMEM((2, tokens, hidden), low),
            pltpu.VMEM((2, tokens, hidden), low),
            pltpu.VMEM((2, tokens, hidden), low),
            pltpu.VMEM((2, tokens, width), low),
            pltpu.VMEM((2, tokens, width), low),
            pltpu.VMEM((width, hidden), full),
            pltpu.VMEM((width, hidden), full),
            pltpu.VMEM((2 * LAYERS, width, LANES), full),
            pltpu.VMEM((LAYERS, 4, 8, width), full),
            pltpu.VMEM((8, 2048), full),
            pltpu.VMEM((2 * LAYERS, 4, 4) + half, low),
            pltpu.VMEM((2 * LAYERS, 3, 4) + half, low),
            pltpu.VMEM((2 * LAYERS, 4) + half, low),
            pltpu.VMEM((2 * LAYERS, 3) + half, low),
            pltpu.VMEM((LAYERS, expand.shape[1], hidden // 2), full),
            pltpu.VMEM((LAYERS,) + half, full),
            pltpu.VMEM((2, SPEC_HALF, LANES), full),
            pltpu.VMEM((2, SPEC_HALF, LANES), low),
            pltpu.VMEM((filters.shape[2], LANES), full),
            pltpu.VMEM((8, LANES), full),
            pltpu.VMEM((8, LANES), full),
            *late_buffers(TILE_ROWS + 16 - 2 * expand.shape[1]),
            *late_buffers(2 * expand.shape[1]),
            sems((GATHERED * 3,)),
            sems((GATHERED * 3,)),
            sems((GATHERED * 12,)),
            sems((GATHERED * 12,)),
            sems((GATHERED * 4,)),
            sems((GATHERED * 4,)),
            sems((48,)),
            sems((48,)),
            sems((5,)),
            sems((5,)),
            sems((LOCAL_SEMS,)),
        ],
        compiler_params=pltpu.CompilerParams(
            collective_id=0, has_side_effects=True, vmem_limit_bytes=VMEM_BYTES
        ),
    )(
        groups, order, keep, images, cotangent, expand, shrink, filters, norms, biases, maps, factors, table
    )


def gelu_pair(values):
    square = values * values
    curve = BEND[4] * square + BEND[3]
    for coefficient in (BEND[2], BEND[1], BEND[0]):
        curve = curve * square + coefficient
    below = 0.5 * jnp.tanh(values * curve) + 0.5
    bell = jnp.exp2(square * (-HALF_LOG2_E) + LOG2_PEAK)
    return values * below, below + values * bell


def normalise(values):
    centred = values - jnp.mean(values, axis=-1, keepdims=True)
    variance = jnp.mean(centred * centred, axis=-1, keepdims=True)
    inv_std = lax.rsqrt(variance + NORM_EPS)
    return centred * inv_std, inv_std


def norm_pull(grad_out, normal, inv_std, gain):
    scaled = grad_out * gain
    return inv_std * (
        scaled
        - jnp.mean(scaled, axis=-1, keepdims=True)
        - normal * jnp.mean(scaled * normal, axis=-1, keepdims=True)
    )


def spans(count, size):
    return [slice(start, start + size) for start in range(0, count, size)]


def stack_rows(pieces):
    return jnp.concatenate(pieces, axis=0)


def row_sums(values):
    return jnp.sum(values.reshape(values.shape[0] // 8, 8, values.shape[1]), axis=0)


def dot(left, right):
    return jnp.dot(left, right, preferred_element_type=jnp.float32)


def dot_low(left, right):
    return dot(left, right).astype(jnp.bfloat16)


def dot_lanes(left, right, kind=jnp.float32):
    return lax.dot_general(
        left, right, (((1,), (1,)), ((), ())), preferred_element_type=jnp.float32
    ).astype(kind)


def dot_rows(left, right):
    return lax.dot_general(
        left, right, (((0,), (0,)), ((), ())), preferred_element_type=jnp.float32
    )


def update_kernel(*refs):
    owner = lax.axis_index("img")
    sources, targets = refs[:20], refs[20:37]
    smalls, output, image_grad = sources[17:20]
    step = pl.program_id(0)
    targets[15][...] = output[...]

    def apply(index, grad, at=(Ellipsis,)):
        values = [ref[at] for ref in sources[3 * index : 3 * index + 3]]
        results = adamw(*values, grad, LEARN_RATES[index], WEIGHT_DECAYS[index])
        for target, result in zip(targets[3 * index : 3 * index + 3], results):
            target[at] = result

    apply(1, sources[15][...])
    apply(2, sources[16][...])
    targets[16][...] = image_grad[...].astype(targets[16].dtype)

    @pl.when(step == 0)
    def _():
        part = sources[0].shape[2]
        bias_part = sources[12].shape[1]
        for layer_id in range(LAYERS):
            for side in range(2):
                start = (2 * layer_id + side) * part
                apply(0, smalls[start : start + part, :BASE], (layer_id, side))
            start = 2 * layer_id * part
            block = jnp.concatenate(
                [smalls[start : start + part], jnp.zeros((LANES - part, LANES), jnp.float32)], axis=0
            )
            apply(3, jnp.transpose(block)[BASE : BASE + 4, :part], (layer_id,))
        window = jnp.concatenate(
            [smalls[TILE_ROWS : TILE_ROWS + 8], smalls[TILE_ROWS + 8 : TILE_ROWS + 16]], axis=1
        )
        offset = owner * bias_part % LANES
        window = pltpu.roll(window, 2 * LANES - offset, 1)
        apply(4, window[:LAYERS, :bias_part])


def update(params, sum_expand, sum_shrink, smalls, output, image_grad):
    steps = 4

    def along(array, axis):
        block = list(array.shape)
        block[axis] //= steps
        return pl.BlockSpec(
            tuple(block), lambda step: tuple(step if k == axis else 0 for k in range(len(block)))
        )

    def whole(array):
        return pl.BlockSpec(array.shape, lambda step: (0,) * array.ndim)

    param_specs = []
    for index, array in enumerate(params):
        kind = index // 3
        param_specs.append(along(array, 3 - kind) if kind in (1, 2) else whole(array))
    image_specs = [along(output, 0), along(image_grad, 0)]
    return pl.pallas_call(
        update_kernel,
        grid=(steps,),
        in_specs=param_specs
        + [along(sum_expand, 2), along(sum_shrink, 1), whole(smalls)]
        + image_specs,
        out_specs=param_specs + image_specs,
        out_shape=[jax.ShapeDtypeStruct(array.shape, jnp.float32) for array in params]
        + [
            jax.ShapeDtypeStruct(output.shape, output.dtype),
            jax.ShapeDtypeStruct(image_grad.shape, jnp.float32),
        ],
        compiler_params=pltpu.CompilerParams(vmem_limit_bytes=VMEM_BYTES),
    )(*params, sum_expand, sum_shrink, smalls, output, image_grad)


def whole_image_body(
    images,
    cotangent,
    image_group,
    row_order,
    keep_mask,
    resample,
    filters,
    filters_first,
    filters_second,
    expand,
    expand_first,
    expand_second,
    shrink,
    shrink_first,
    shrink_second,
    norm_params,
    norm_first,
    norm_second,
    mlp_bias,
    bias_first,
    bias_second,
):
    count, rows, _, width = images.shape
    low = jnp.bfloat16
    factors = np.zeros((3, SPEC_HALF, LANES), np.float32)
    factors[:2, : rows * HALF] = np.tile(slot_weights(), (1, rows))[:, :, None]
    for index in range(4):
        factors[2, rows * HALF + index, BASE + index] = 1.0
    table = natural_tables(2).transpose(0, 2, 1).reshape(2, SIDE, SIDE, 2 * SPEC_ROWS)
    filter_group = [
        array.transpose(0, 2, 3, 1) for array in (filters, filters_first, filters_second)
    ]
    sum_expand, sum_shrink, small_sums, output, image_grad, _ = train(
        image_group,
        row_order,
        keep_mask.transpose(1, 2, 0),
        images,
        cotangent,
        expand,
        shrink,
        filter_group[0],
        norm_params,
        mlp_bias,
        resample.transpose(1, 2, 0, 3),
        jnp.asarray(factors),
        jnp.asarray(table),
    )
    results = update(
        filter_group
        + [expand, expand_first, expand_second]
        + [shrink, shrink_first, shrink_second]
        + [norm_params, norm_first, norm_second]
        + [mlp_bias, bias_first, bias_second],
        sum_expand,
        sum_shrink,
        small_sums,
        output,
        image_grad,
    )
    new_filters = [array.transpose(0, 3, 1, 2) for array in results[:3]]
    return (results[15], results[16], *new_filters, *results[3:15])


def solution(mesh):
    paired = mesh.shape["grid"] == 2 and mesh.shape["img"] == 16
    return jax.shard_map(
        whole_image_body if paired else body,
        mesh=mesh,
        in_specs=(
            P("img", "grid", None, None),
            P("img", "grid", None, None),
            P("img"),
            P(),
            P("img", None, None),
            P(None, "grid", None, None),
            P(None, None, None, "img"),
            P(None, None, None, "img"),
            P(None, None, None, "img"),
            P(None, "img", None),
            P(None, "img", None),
            P(None, "img", None),
            P(None, "img", None),
            P(None, "img", None),
            P(None, "img", None),
            P(None, None, "img"),
            P(None, None, "img"),
            P(None, None, "img"),
            P(None, "img"),
            P(None, "img"),
            P(None, "img"),
        ),
        out_specs=(
            P("img", "grid", None, None),
            P("img", "grid", None, None),
            P(None, None, None, "img"),
            P(None, None, None, "img"),
            P(None, None, None, "img"),
            P(None, "img", None),
            P(None, "img", None),
            P(None, "img", None),
            P(None, "img", None),
            P(None, "img", None),
            P(None, "img", None),
            P(None, None, "img"),
            P(None, None, "img"),
            P(None, None, "img"),
            P(None, "img"),
            P(None, "img"),
            P(None, "img"),
        ),
        check_vma=False,
    )
```
